256 devices in a mesh: ctx: 128 (over y, x, z_lo, core), tp: 2 (over z_hi).
Axes of the slice: x: 4, y: 4, z: 8 (z_hi: 2, z_lo: 4; z = z_hi * 4 + z_lo), core: 2. Of those that a mesh axis runs over, the one named last changes fastest.
Arguments:
- query_proj: bfloat16 [16384, 4096], P('ctx', 'tp'), may hold values from -6 to 6
- key_proj: bfloat16 [16384, 4096], P('ctx', 'tp'), may hold values from -6 to 6
- value_proj: bfloat16 [16384, 4096], P('ctx', 'tp'), may hold values from -6 to 6
- out_grad: bfloat16 [16384, 4096], P('ctx', 'tp'), may hold values from -6 to 6
- raw_filter: bfloat16 [16384, 2048], P('ctx'), may hold values from -6 to 6
Outputs:
- query_grad: bfloat16 [16384, 4096], P('ctx', 'tp')
- key_grad: bfloat16 [16384, 4096], P('ctx', 'tp')
- value_grad: bfloat16 [16384, 4096], P('ctx', 'tp')
- filter_grad: bfloat16 [16384, 2048], P('ctx')
The draws below stay inside these ranges and needn't reach their ends.
All inputs are finite; a program needn't handle non-finite values.
Results may differ from the reference program's by a relative error of at most 0.0057.
Values may be sent and summed in bfloat16 or wider, within the bound.
A program may use at most 128 MiB of HBM per device.

```python
import math
import jax
import jax.numpy as jnp
from jax import lax

C = 4096
SEQ = 16384
FILTERS = 2048


def shard_levels(stream_key, extent, pieces, smallest, top_value):
    gain = 1.0
    for dim, blocks in pieces:
        heights = jax.random.uniform(jax.random.fold_in(jax.random.fold_in(stream_key, 6), dim), (blocks,), jnp.float32, smallest / len(pieces), top_value / len(pieces))
        gain = gain * jnp.repeat(jnp.exp(heights), extent[dim] // blocks).reshape((-1,) + (1,) * (len(extent) - 1 - dim))
    return gain


def normal_values(own_key, extent, scale, reach, pieces=(), kind=jnp.bfloat16):
    result = scale * jax.random.normal(own_key, extent, jnp.float32)
    if pieces:
        result = result * shard_levels(own_key, extent, pieces, -0.22, 0.18)
    return jnp.clip(result, -reach, reach).astype(kind)


def setup_inputs(seed: int = 0) -> dict:
    key_of = jax.random.split(jax.random.key(seed), 6)
    return {
        "query_proj": normal_values(key_of[0], (SEQ, C), 1.0, 6.0, ((0, 128), (1, 2))),
        "key_proj": normal_values(key_of[1], (SEQ, C), 1.0, 6.0, ((0, 128), (1, 2))),
        "value_proj": normal_values(key_of[2], (SEQ, C), 1.0, 6.0, ((0, 128), (1, 2))),
        "out_grad": normal_values(key_of[3], (SEQ, C), 1.0, 6.0, ((0, 128), (1, 2))),
        "raw_filter": normal_values(key_of[4], (SEQ, FILTERS), 1.0, 6.0, ((0, 128),)),
    }


def reference(query_proj, key_proj, value_proj, out_grad, raw_filter):
    pair_product = (query_proj.astype(jnp.float32) * key_proj.astype(jnp.float32)).astype(jnp.bfloat16)
    gate_grad = (out_grad.astype(jnp.float32) * value_proj.astype(jnp.float32)).astype(jnp.bfloat16)
    scale = SEQ ** -0.5
    filt = raw_filter.astype(jnp.float32) * scale
    filt_all = jnp.concatenate([filt, filt], axis=1)
    block_width = math.gcd(C, 256)
    block_count = C // block_width

    def to_blocks(array):
        return array.astype(jnp.float32).reshape(SEQ, block_count, block_width).transpose(1, 0, 2)

    def from_blocks(array):
        return array.transpose(1, 0, 2).reshape(SEQ, C)

    def one_block(items):
        prod_block, grad_block, filt_block = items
        padded_len = 2 * SEQ
        prod_spec = jnp.fft.rfft(prod_block, n=padded_len, axis=0)
        grad_spec = jnp.fft.rfft(grad_block, n=padded_len, axis=0)
        filt_spec = jnp.fft.rfft(filt_block, n=padded_len, axis=0)
        conv = jnp.fft.irfft(filt_spec * prod_spec, n=padded_len, axis=0)[:SEQ]
        conv_grad = jnp.fft.irfft(jnp.conj(filt_spec) * grad_spec, n=padded_len, axis=0)[:SEQ]
        lag_sum = jnp.fft.irfft(jnp.conj(prod_spec) * grad_spec, n=padded_len, axis=0)[:SEQ]
        return conv.astype(jnp.float32), conv_grad.astype(jnp.float32), lag_sum.astype(jnp.float32)

    conv, conv_grad, lag_sum = lax.map(one_block, (to_blocks(pair_product), to_blocks(gate_grad), to_blocks(filt_all)))
    conv = from_blocks(conv).astype(jnp.bfloat16)
    conv_grad = from_blocks(conv_grad).astype(jnp.bfloat16)
    lag_sum = from_blocks(lag_sum)
    filter_grad = ((lag_sum[:, :FILTERS] + lag_sum[:, FILTERS:]) * scale).astype(jnp.bfloat16)
    query_grad = (conv_grad.astype(jnp.float32) * key_proj.astype(jnp.float32)).astype(jnp.bfloat16)
    key_grad = (conv_grad.astype(jnp.float32) * query_proj.astype(jnp.float32)).astype(jnp.bfloat16)
    value_grad = (out_grad.astype(jnp.float32) * conv.astype(jnp.float32)).astype(jnp.bfloat16)
    return query_grad, key_grad, value_grad, filter_grad
```

```python
import functools
import math

import jax
import jax.numpy as jnp
import ml_dtypes
import numpy as np
from jax import lax
from jax.experimental import pallas as pl
from jax.experimental.pallas import tpu as pltpu
from jax.sharding import PartitionSpec as P

MESH = pl.DeviceIdType.MESH
BF16 = jnp.bfloat16
F32 = jnp.float32

BLOCK = 128
LONG = 256
PERIOD = BLOCK * LONG
COLS = 16
DEPTH = 16
OWN = 8


def split_table(table):
    high = table.astype(ml_dtypes.bfloat16)
    low = (table - high.astype(np.float64)).astype(ml_dtypes.bfloat16)
    return high, low


def tables():
    freq = np.arange(LONG)[:, None]
    block = np.arange(BLOCK)[None, :]
    long_angle = 2.0 * math.pi * ((freq * block) % LONG) / LONG
    cos_long, sin_long = np.cos(long_angle), np.sin(long_angle)
    outer = np.block([[cos_long, sin_long], [-sin_long, cos_long]])
    small_angle = 2.0 * math.pi * ((block.T * block) % BLOCK) / BLOCK
    cos_small, sin_small = np.cos(small_angle), np.sin(small_angle)
    inner = np.block([[cos_small, -sin_small], [sin_small, cos_small]])
    twid_angle = 2.0 * math.pi * (freq * block) / PERIOD
    twid_cos = np.cos(twid_angle).astype(np.float32)
    twid_sin = np.sin(twid_angle).astype(np.float32)
    return (
        *split_table(outer),
        *split_table(inner),
        *split_table(inner.T),
        *split_table(outer.T),
        twid_cos,
        twid_sin,
    )


def mul(left, right):
    return jnp.dot(left, right, preferred_element_type=F32)


def halves(value):
    high = value.astype(BF16)
    return high, (value - high.astype(F32)).astype(BF16)


def kernel(
    q_ref, k_ref, v_ref, g_ref, f_ref,
    out_hi, out_lo, in_hi, in_lo, back_hi, back_lo, last_hi, last_lo, cos_ref, sin_ref,
    dq_ref, dk_ref, dv_ref, df_ref,
    cut_f, cut_p, cut_g, mid_f, mid_p, mid_g, got_f, got_p, got_g,
    send_c, send_d, send_l, half_c, half_d, half_l, end_c, end_d, end_l,
    wide, spec_h, spec_p,
    z_send, z_recv, xy_send, xy_recv, loc,
):
    ctx, tp = lax.axis_index("ctx"), lax.axis_index("tp")
    col = ctx // 8
    low = ctx % 8
    zc = tp * 8 + low
    z, core = zc // 2, zc % 2

    def in_column(index):
        return (col * 8 + index % 8, index // 8)

    def in_plane(index):
        return (index * 8 + low, tp)

    def around(step):
        return lax.rem(zc + step, DEPTH)

    def beside(step):
        across = lax.rem(col % 4 + step % 4, 4)
        along = lax.rem(col // 4 + step // 4, 4)
        return along * 4 + across

    barrier = pltpu.get_barrier_semaphore()

    def greet(step, carry):
        pl.semaphore_signal(barrier, inc=1, device_id=in_column(around(step)), device_id_type=MESH)
        pl.semaphore_signal(barrier, inc=1, device_id=in_plane(beside(step)), device_id_type=MESH)
        return carry

    lax.fori_loop(1, 16, greet, 0)

    def z_copy(kind, src, dst, index):
        return pltpu.make_async_remote_copy(
            src_ref=src, dst_ref=dst, send_sem=z_send.at[kind], recv_sem=z_recv.at[kind],
            device_id=in_column(index), device_id_type=MESH,
        )

    def xy_copy(kind, src, dst, index):
        return pltpu.make_async_remote_copy(
            src_ref=src, dst_ref=dst, send_sem=xy_send.at[kind], recv_sem=xy_recv.at[kind],
            device_id=in_plane(index), device_id_type=MESH,
        )

    def columns(index):
        return pl.ds(pl.multiple_of(index * BLOCK, BLOCK), BLOCK)

    def turned(block):
        return block.T.astype(BF16).reshape(COLS, OWN, BLOCK)

    def cut_filter(step, carry):
        index = around(step)
        cut_f[index] = turned(f_ref[:, columns(index)].astype(F32))
        return carry

    lax.fori_loop(0, DEPTH, cut_filter, 0)
    pl.semaphore_wait(barrier, 30)
    flip = lax.rem(col // 4 + col + core, 2)

    def send_filter(step, carry):
        turn = step // 2
        away = jnp.where(turn == 3, jnp.where(flip == 0, 2, 6), jnp.where(turn == 2, 7, turn))
        index = lax.rem(z + away, 8) * 2 + lax.rem(core + step, 2)
        z_copy(0, cut_f.at[index], mid_f.at[low], index).start()
        return carry

    lax.fori_loop(1, 8, send_filter, 0)
    own_f = pltpu.make_async_copy(cut_f.at[zc], mid_f.at[low], loc.at[0])
    own_f.start()

    def cut_product(kind, left, right, cut, mid):
        def one(step, carry):
            index = around(step)
            cols = columns(index)
            product = left[:, cols].astype(F32) * right[:, cols].astype(F32)
            cut[index] = turned(product.astype(BF16).astype(F32))
            z_copy(kind, cut.at[index], mid.at[zc], index).start()
            return carry

        lax.fori_loop(1, DEPTH, one, 0)
        cols = columns(zc)
        product = left[:, cols].astype(F32) * right[:, cols].astype(F32)
        mid[zc] = turned(product.astype(BF16).astype(F32))

    cut_product(1, q_ref, k_ref, cut_p, mid_p)
    cut_product(2, g_ref, v_ref, cut_g, mid_g)

    def z_done(kind, mid, count):
        part = mid.at[pl.ds(0, count)]
        z_copy(kind, part, part, around(1)).wait_recv()

    def cross(kind, mid, got):
        def one(step, carry):
            index = beside(step)
            xy_copy(kind, mid.at[:, index], got.at[col], index).start()
            return carry

        lax.fori_loop(1, COLS, one, 0)
        own = pltpu.make_async_copy(mid.at[:, col], got.at[col], loc.at[kind])
        own.start()
        return own

    def xy_done(kind, got, own):
        own.wait()
        part = got.at[pl.ds(0, COLS - 1)]
        xy_copy(kind, part, part, beside(1)).wait_recv()

    cos, sin = cos_ref[...], sin_ref[...]
    cos2 = jnp.concatenate([cos, cos], axis=1)
    sin2 = jnp.concatenate([sin, sin], axis=1)

    def forward(sig, depth):
        first = mul(out_hi[:, :depth], sig) + mul(out_lo[:, :depth], sig)
        real, imag = first[:LONG], first[LONG:]
        tr = real * cos2 + imag * sin2
        ti = imag * cos2 - real * sin2
        rows = jnp.concatenate(
            [
                jnp.concatenate([tr[:, :BLOCK], ti[:, :BLOCK]], axis=1),
                jnp.concatenate([tr[:, BLOCK:], ti[:, BLOCK:]], axis=1),
            ],
            axis=0,
        )
        hi, lo = halves(rows)
        return mul(hi, in_hi[...]) + mul(hi, in_lo[...]) + mul(lo, in_hi[...])

    def inverse(spec, rows):
        hi, lo = halves(spec)
        mixed = mul(hi, back_hi[...]) + mul(hi, back_lo[...]) + mul(lo, back_hi[...])
        real = jnp.concatenate([mixed[:LONG, :BLOCK], mixed[LONG:, :BLOCK]], axis=1)
        imag = jnp.concatenate([mixed[:LONG, BLOCK:], mixed[LONG:, BLOCK:]], axis=1)
        both = jnp.concatenate([real * cos2 - imag * sin2, real * sin2 + imag * cos2], axis=0)
        hi, lo = halves(both)
        total = (
            mul(last_hi[:rows], hi) + mul(last_lo[:rows], hi) + mul(last_hi[:rows], lo)
        )
        return total * (1.0 / PERIOD / BLOCK)

    def times(left, right, conjugate):
        lr, li = left[:, :BLOCK], left[:, BLOCK:]
        rr, ri = right[:, :BLOCK], right[:, BLOCK:]
        if conjugate:
            return jnp.concatenate([lr * rr + li * ri, lr * ri - li * rr], axis=1)
        return jnp.concatenate([lr * rr - li * ri, lr * ri + li * rr], axis=1)

    def load(base, jump):
        parts = [wide[pl.ds(base + n * jump, 8, stride=OWN), :] for n in range(COLS)]
        return jnp.concatenate(parts, axis=0).astype(BF16)

    def store(base, jump, value):
        for n in range(COLS):
            wide[pl.ds(base + n * jump, 8, stride=OWN), :] = value[n * 8 : n * 8 + 8]

    def load_pair(one):
        top = [load(one, BLOCK), load(one + 1, BLOCK)]
        bottom = [load(one + 64, BLOCK), load(one + 65, BLOCK)]
        return jnp.concatenate(
            [jnp.concatenate(top, axis=1), jnp.concatenate(bottom, axis=1)], axis=0
        )

    def store_pair(one, value):
        store(one, BLOCK, value[:BLOCK, :BLOCK])
        store(one + 1, BLOCK, value[:BLOCK, BLOCK:])
        store(one + 64, BLOCK, value[BLOCK:, :BLOCK])
        store(one + 65, BLOCK, value[BLOCK:, BLOCK:])

    def spread(got):
        rows = got.shape[0] * got.shape[1] * OWN
        wide[pl.ds(0, rows), :] = got[...].astype(F32).reshape(rows, BLOCK)

    def gather(out):
        rows = out.shape[0] * out.shape[1] * OWN
        out[...] = wide[pl.ds(0, rows), :].astype(BF16).reshape(out.shape)

    own_f.wait()
    z_done(0, mid_f, 7)
    side_f = cross(0, mid_f, got_f)
    xy_done(0, got_f, side_f)
    spread(got_f)

    def filter_spectrum(pair, carry):
        one = 2 * pair
        sig = jnp.concatenate([load(one, 64), load(one + 1, 64)], axis=1)
        spec_h[pair] = forward(sig, BLOCK)
        return carry

    lax.fori_loop(0, OWN // 2, filter_spectrum, 0)

    z_done(1, mid_p, DEPTH - 1)
    side_p = cross(1, mid_p, got_p)
    xy_done(1, got_p, side_p)
    spread(got_p)

    def convolve(pair, carry):
        spec = forward(load_pair(2 * pair), 2 * BLOCK)
        spec_p[pair] = spec
        store_pair(2 * pair, inverse(times(spec_h[pair], spec, False), 2 * BLOCK))
        return carry

    lax.fori_loop(0, OWN // 2, convolve, 0)
    gather(send_c)

    def deliver(kind, out, mid):
        def one(step, carry):
            index = around(step)
            where = lax.rem(index, out.shape[1])
            z_copy(kind, out.at[:, where], mid.at[zc], index).start()
            return carry

        lax.fori_loop(1, DEPTH, one, 0)
        own = pltpu.make_async_copy(out.at[:, lax.rem(zc, out.shape[1])], mid.at[zc], loc.at[kind + 3])
        own.start()
        return own

    z_done(2, mid_g, DEPTH - 1)
    side_g = cross(2, mid_g, got_g)
    own_c = deliver(3, send_c, half_c)

    xy_done(2, got_g, side_g)
    spread(got_g)

    def correlate(pair, carry):
        spec = forward(load_pair(2 * pair), 2 * BLOCK)
        store_pair(2 * pair, inverse(times(spec_h[pair], spec, True), 2 * BLOCK))
        spec_p[pair] = times(spec_p[pair], spec, True)
        return carry

    lax.fori_loop(0, OWN // 2, correlate, 0)
    gather(send_d)
    own_d = deliver(4, send_d, half_d)

    def lag(pair, carry):
        value = inverse(spec_p[pair], BLOCK)
        store(2 * pair, 64, value[:, :BLOCK])
        store(2 * pair + 1, 64, value[:, BLOCK:])
        return carry

    lax.fori_loop(0, OWN // 2, lag, 0)
    gather(send_l)
    own_l = deliver(5, send_l, half_l)

    own_c.wait()
    z_done(3, half_c, DEPTH - 1)
    side_c = cross(3, half_c, end_c)
    xy_done(3, end_c, side_c)

    def home(end, index):
        return end[:, index].astype(F32).reshape(BLOCK, BLOCK).T

    def finish_value(index, carry):
        cols = columns(index)
        dv_ref[:, cols] = (home(end_c, index) * g_ref[:, cols].astype(F32)).astype(BF16)
        return carry

    lax.fori_loop(0, DEPTH, finish_value, 0)

    own_d.wait()
    z_done(4, half_d, DEPTH - 1)
    side_d = cross(4, half_d, end_d)
    xy_done(4, end_d, side_d)

    def finish_gates(index, carry):
        cols = columns(index)
        back = home(end_d, index)
        dq_ref[:, cols] = (back * k_ref[:, cols].astype(F32)).astype(BF16)
        dk_ref[:, cols] = (back * q_ref[:, cols].astype(F32)).astype(BF16)
        return carry

    lax.fori_loop(0, DEPTH, finish_gates, 0)

    own_l.wait()
    z_done(5, half_l, DEPTH - 1)
    side_l = cross(5, half_l, end_l)
    xy_done(5, end_l, side_l)

    def finish_filter(index, carry):
        df_ref[:, columns(index)] = home(end_l, index).astype(BF16)
        return carry

    lax.fori_loop(0, DEPTH, finish_filter, 0)

    for kind in range(6):
        part = mid_f.at[pl.ds(0, 7)] if kind == 0 else mid_p.at[pl.ds(0, DEPTH - 1)]
        z_copy(kind, part, part, around(1)).wait_send()
        part = (got_f if kind == 0 else got_p).at[pl.ds(0, COLS - 1)]
        xy_copy(kind, part, part, beside(1)).wait_send()


def per_device(query_proj, key_proj, value_proj, out_grad, raw_filter):
    shape = jax.ShapeDtypeStruct(query_proj.shape, BF16)
    full = pltpu.VMEM((COLS, DEPTH, OWN, BLOCK), BF16)
    half = pltpu.VMEM((COLS, DEPTH // 2, OWN, BLOCK), BF16)
    near = pltpu.VMEM((DEPTH // 2, COLS, OWN, BLOCK), BF16)
    consts = tuple(jnp.asarray(table) for table in tables())
    vmem = pl.BlockSpec(memory_space=pltpu.VMEM)
    return pl.pallas_call(
        kernel,
        out_shape=(shape,) * 4,
        in_specs=[vmem] * (5 + len(consts)),
        out_specs=(vmem,) * 4,
        scratch_shapes=[
            full, full, full, near, full, full, half, full, full,
            full, full, half, full, full, full, full, full, full,
            pltpu.VMEM((COLS * DEPTH * OWN, BLOCK), F32),
            pltpu.VMEM((OWN // 2, 2 * LONG, 2 * BLOCK), F32),
            pltpu.VMEM((OWN // 2, 2 * LONG, 2 * BLOCK), F32),
            pltpu.SemaphoreType.DMA((6,)),
            pltpu.SemaphoreType.DMA((6,)),
            pltpu.SemaphoreType.DMA((6,)),
            pltpu.SemaphoreType.DMA((6,)),
            pltpu.SemaphoreType.DMA((9,)),
        ],
        compiler_params=pltpu.CompilerParams(
            collective_id=0, has_side_effects=True, vmem_limit_bytes=56 * 1024 * 1024
        ),
    )(query_proj, key_proj, value_proj, out_grad, raw_filter, *consts)


def solution(mesh):
    in_specs = (P("ctx", "tp"), P("ctx", "tp"), P("ctx", "tp"), P("ctx", "tp"), P("ctx", None))
    out_specs = (P("ctx", "tp"), P("ctx", "tp"), P("ctx", "tp"), P("ctx", None))
    return jax.shard_map(
        per_device, mesh=mesh, in_specs=in_specs, out_specs=out_specs, check_vma=False
    )
```

```python
import functools
import math

import jax
import jax.numpy as jnp
import ml_dtypes
import numpy as np
from jax import lax
from jax.experimental import pallas as pl
from jax.experimental.pallas import tpu as pltpu
from jax.sharding import PartitionSpec as P

MESH = pl.DeviceIdType.MESH
BF16 = jnp.bfloat16
F32 = jnp.float32

BLOCK = 128
LONG = 256
PERIOD = BLOCK * LONG
COLS = 16
DEPTH = 16
OWN = 8


def split_table(table):
    high = table.astype(ml_dtypes.bfloat16)
    low = (table - high.astype(np.float64)).astype(ml_dtypes.bfloat16)
    return np.stack([high, low])


def tables():
    freq = np.arange(LONG)[:, None]
    block = np.arange(BLOCK)[None, :]
    long_angle = 2.0 * math.pi * ((freq * block) % LONG) / LONG
    cos_long, sin_long = np.cos(long_angle), np.sin(long_angle)
    outer = np.block([[cos_long, sin_long], [-sin_long, cos_long]])
    small_angle = 2.0 * math.pi * ((block.T * block) % BLOCK) / BLOCK
    cos_small, sin_small = np.cos(small_angle), np.sin(small_angle)
    inner = np.block([[cos_small, -sin_small], [sin_small, cos_small]])
    twid_angle = 2.0 * math.pi * (freq * block) / PERIOD
    turn = np.stack([np.cos(twid_angle), np.sin(twid_angle)]).astype(np.float32)
    return (*(split_table(table) for table in (outer, inner, inner.T, outer.T)), turn)


def mul(left, right):
    return jnp.dot(left, right, preferred_element_type=F32)


def halves(value):
    high = value.astype(BF16)
    return high, (value - high.astype(F32)).astype(BF16)


def kernel(
    q_in, k_in, v_in, g_in, f_in, out_in, inn_in, back_in, last_in, turn_in,
    dq_out, dk_out, dv_out, df_out,
    q_ref, k_ref, v_ref, g_ref, f_ref, out_tab, inn_tab, back_tab, last_tab, turn_tab,
    dq_ref, dk_ref, dv_ref, df_ref,
    cut_f, mid_f, got_f, cut_p, got_p, cut_g, got_g,
    send_c, half_c, end_c, send_d, half_d, end_d, send_l, end_l,
    wide, spec_h, spec_p,
    z_send, z_recv, xy_send, xy_recv, far_send, far_recv, loc, fetch, leave, ready,
):
    ctx, tp = lax.axis_index("ctx"), lax.axis_index("tp")
    col = ctx // 8
    low = ctx % 8
    zc = tp * 8 + low
    z, core = zc // 2, zc % 2
    me = col * DEPTH + zc

    def device(there, depth):
        return (there * 8 + depth % 8, depth // 8)

    def around(step):
        return lax.rem(zc + step, DEPTH)

    def beside(step):
        across = lax.rem(col % 4 + step % 4, 4)
        along = lax.rem(col // 4 + step // 4, 4)
        return along * 4 + across

    depths = [around(step) for step in range(DEPTH)]
    barrier = pltpu.get_barrier_semaphore()

    def greet(step, carry):
        for target in (device(col, around(step)), device(beside(step), zc)):
            pl.semaphore_signal(barrier, inc=1, device_id=target, device_id_type=MESH)
        return carry

    lax.fori_loop(1, 16, greet, 0)

    arrivals = [
        pltpu.make_async_copy(src, dst, fetch.at[n])
        for n, (src, dst) in enumerate(
            (
                (f_in, f_ref), (q_in, q_ref), (k_in, k_ref), (g_in, g_ref), (v_in, v_ref),
                (out_in, out_tab), (inn_in, inn_tab), (back_in, back_tab),
                (last_in, last_tab), (turn_in, turn_tab),
            )
        )
    ]
    for copy in arrivals:
        copy.start()

    def z_copy(kind, src, dst, index):
        return pltpu.make_async_remote_copy(
            src_ref=src, dst_ref=dst, send_sem=z_send.at[kind], recv_sem=z_recv.at[kind],
            device_id=device(col, index), device_id_type=MESH,
        )

    def xy_copy(kind, src, dst, index):
        return pltpu.make_async_remote_copy(
            src_ref=src, dst_ref=dst, send_sem=xy_send.at[kind], recv_sem=xy_recv.at[kind],
            device_id=device(index, zc), device_id_type=MESH,
        )

    def far_copy(kind, src, dst, there, depth):
        return pltpu.make_async_remote_copy(
            src_ref=src, dst_ref=dst, send_sem=far_send.at[kind], recv_sem=far_recv.at[kind],
            device_id=device(there, depth), device_id_type=MESH,
        )

    def columns(index):
        return pl.ds(pl.multiple_of(index * BLOCK, BLOCK), BLOCK)

    def turned(block):
        return block.T.astype(BF16).reshape(DEPTH, OWN, BLOCK)

    arrivals[0].wait()

    def cut_filter(index, carry):
        cut_f[index] = turned(f_ref[:, columns(index)].astype(F32))
        return carry

    lax.fori_loop(0, COLS, cut_filter, 0)
    pl.semaphore_wait(barrier, 30)

    def announce(step, carry):
        target = device(beside(step), zc)
        pl.semaphore_signal(ready, inc=1, device_id=target, device_id_type=MESH)
        return carry

    lax.fori_loop(1, COLS, announce, 0)
    flip = lax.rem(col // 4 + col + core, 2)

    def send_filter(step, carry):
        turn = step // 2
        away = jnp.where(turn == 3, jnp.where(flip == 0, 2, 6), jnp.where(turn == 2, 7, turn))
        index = lax.rem(z + away, 8) * 2 + lax.rem(core + step, 2)
        z_copy(0, cut_f.at[:, index], mid_f.at[low], index).start()
        return carry

    lax.fori_loop(1, 8, send_filter, 0)
    own_f = pltpu.make_async_copy(cut_f.at[:, zc], mid_f.at[low], loc.at[0])
    own_f.start()

    def cut_block(kind, step, left, right, cut, got):
        there = beside(step)
        cols = columns(there)
        product = left[:, cols].astype(F32) * right[:, cols].astype(F32)
        cut[pl.ds(there * DEPTH, DEPTH)] = turned(product.astype(BF16).astype(F32))
        return there

    def send_block(kind, there, depths, cut, got):
        for depth in depths:
            far_copy(kind, cut.at[there * DEPTH + depth], got.at[me], there, depth).start()

    def cut_product(kind, left, right, cut, got, before):
        there = cut_block(kind, 0, left, right, cut, got)
        send_block(kind, there, depths[1:], cut, got)
        before()

        def one(step, carry):
            there = cut_block(kind, step, left, right, cut, got)
            send_block(kind, there, depths, cut, got)
            return carry

        lax.fori_loop(1, COLS, one, 0)
        own = pltpu.make_async_copy(cut.at[me], got.at[me], loc.at[kind + 1])
        own.start()
        return own

    def far_done(kind, got, own):
        own.wait()
        part = got.at[pl.ds(0, COLS * DEPTH - 1)]
        far_copy(kind, part, part, col, depths[1]).wait_recv()

    def z_done(kind, mid, count):
        part = mid.at[pl.ds(0, count)]
        z_copy(kind, part, part, depths[1]).wait_recv()

    def cross(kind, mid, got):
        def one(step, carry):
            index = beside(step)
            xy_copy(kind, mid.at[:, index], got.at[col], index).start()
            return carry

        lax.fori_loop(1, COLS, one, 0)
        own = pltpu.make_async_copy(mid.at[:, col], got.at[col], loc.at[kind + 3])
        own.start()
        return own

    def xy_done(kind, got, own):
        own.wait()
        part = got.at[pl.ds(0, COLS - 1)]
        xy_copy(kind, part, part, beside(1)).wait_recv()

    arrivals[1].wait()
    arrivals[2].wait()
    own_p = cut_product(0, q_ref, k_ref, cut_p, got_p, lambda: pl.semaphore_wait(ready, COLS - 1))
    own_f.wait()
    z_done(0, mid_f, 7)
    side_f = cross(0, mid_f, got_f)
    arrivals[3].wait()
    arrivals[4].wait()
    own_g = cut_product(1, g_ref, v_ref, cut_g, got_g, lambda: None)
    for copy in arrivals[5:]:
        copy.wait()

    cos, sin = turn_tab[0], turn_tab[1]
    cos2 = jnp.concatenate([cos, cos], axis=1)
    sin2 = jnp.concatenate([sin, sin], axis=1)

    def forward(sig, depth):
        first = mul(out_tab[0, :, :depth], sig) + mul(out_tab[1, :, :depth], sig)
        real, imag = first[:LONG], first[LONG:]
        tr = real * cos2 + imag * sin2
        ti = imag * cos2 - real * sin2
        rows = jnp.concatenate(
            [
                jnp.concatenate([tr[:, :BLOCK], ti[:, :BLOCK]], axis=1),
                jnp.concatenate([tr[:, BLOCK:], ti[:, BLOCK:]], axis=1),
            ],
            axis=0,
        )
        hi, lo = halves(rows)
        return mul(hi, inn_tab[0]) + mul(hi, inn_tab[1]) + mul(lo, inn_tab[0])

    def inverse(spec, rows):
        hi, lo = halves(spec)
        mixed = mul(hi, back_tab[0]) + mul(hi, back_tab[1]) + mul(lo, back_tab[0])
        real = jnp.concatenate([mixed[:LONG, :BLOCK], mixed[LONG:, :BLOCK]], axis=1)
        imag = jnp.concatenate([mixed[:LONG, BLOCK:], mixed[LONG:, BLOCK:]], axis=1)
        both = jnp.concatenate([real * cos2 - imag * sin2, real * sin2 + imag * cos2], axis=0)
        hi, lo = halves(both)
        total = (
            mul(last_tab[0, :rows], hi) + mul(last_tab[1, :rows], hi) + mul(last_tab[0, :rows], lo)
        )
        return total * (1.0 / PERIOD / BLOCK)

    def times(left, right, conjugate):
        lr, li = left[:, :BLOCK], left[:, BLOCK:]
        rr, ri = right[:, :BLOCK], right[:, BLOCK:]
        if conjugate:
            return jnp.concatenate([lr * rr + li * ri, lr * ri - li * rr], axis=1)
        return jnp.concatenate([lr * rr - li * ri, lr * ri + li * rr], axis=1)

    def load(base, jump):
        parts = [wide[pl.ds(base + n * jump, 8, stride=OWN), :] for n in range(COLS)]
        return jnp.concatenate(parts, axis=0).astype(BF16)

    def store(base, jump, value):
        for n in range(COLS):
            wide[pl.ds(base + n * jump, 8, stride=OWN), :] = value[n * 8 : n * 8 + 8]

    def load_pair(one):
        top = [load(one, BLOCK), load(one + 1, BLOCK)]
        bottom = [load(one + 64, BLOCK), load(one + 65, BLOCK)]
        return jnp.concatenate(
            [jnp.concatenate(top, axis=1), jnp.concatenate(bottom, axis=1)], axis=0
        )

    def store_pair(one, value):
        store(one, BLOCK, value[:BLOCK, :BLOCK])
        store(one + 1, BLOCK, value[:BLOCK, BLOCK:])
        store(one + 64, BLOCK, value[BLOCK:, :BLOCK])
        store(one + 65, BLOCK, value[BLOCK:, BLOCK:])

    def spread(got):
        value = got[...].astype(F32)
        rows = value.size // BLOCK
        wide[pl.ds(0, rows), :] = value.reshape(rows, BLOCK)

    def gather(out):
        rows = out.shape[0] * out.shape[1] * OWN
        out[...] = wide[pl.ds(0, rows), :].astype(BF16).reshape(out.shape)

    xy_done(0, got_f, side_f)
    spread(got_f)

    def filter_spectrum(pair, carry):
        one = 2 * pair
        sig = jnp.concatenate([load(one, 64), load(one + 1, 64)], axis=1)
        spec_h[pair] = forward(sig, BLOCK)
        return carry

    lax.fori_loop(0, OWN // 2, filter_spectrum, 0)

    far_done(0, got_p, own_p)
    spread(got_p)

    def convolve(pair, carry):
        spec = forward(load_pair(2 * pair), 2 * BLOCK)
        spec_p[pair] = spec
        store_pair(2 * pair, inverse(times(spec_h[pair], spec, False), 2 * BLOCK))
        return carry

    lax.fori_loop(0, OWN // 2, convolve, 0)
    gather(send_c)

    def deliver(kind, out, mid):
        def one(step, carry):
            index = around(step)
            z_copy(kind, out.at[:, index], mid.at[zc], index).start()
            return carry

        lax.fori_loop(1, DEPTH, one, 0)
        own = pltpu.make_async_copy(out.at[:, zc], mid.at[zc], loc.at[kind + 5])
        own.start()
        return own

    own_c = deliver(1, send_c, half_c)

    far_done(1, got_g, own_g)
    spread(got_g)

    def correlate(pair, carry):
        spec = forward(load_pair(2 * pair), 2 * BLOCK)
        store_pair(2 * pair, inverse(times(spec_h[pair], spec, True), 2 * BLOCK))
        spec_p[pair] = times(spec_p[pair], spec, True)
        return carry

    lax.fori_loop(0, OWN // 2, correlate, 0)
    gather(send_d)
    own_d = deliver(2, send_d, half_d)

    def lag(pair, carry):
        value = inverse(spec_p[pair], BLOCK)
        store(2 * pair, 64, value[:, :BLOCK])
        store(2 * pair + 1, 64, value[:, BLOCK:])
        return carry

    lax.fori_loop(0, OWN // 2, lag, 0)
    gather(send_l)

    def send_lag(there, depths):
        for depth in depths:
            far_copy(2, send_l.at[there, depth % 8], end_l.at[me], there, depth).start()

    def deliver_lag(step, carry):
        send_lag(beside(step), depths)
        return carry

    send_lag(col, depths[1:])
    lax.fori_loop(1, COLS, deliver_lag, 0)
    own_l = pltpu.make_async_copy(send_l.at[col, low], end_l.at[me], loc.at[8])
    own_l.start()

    own_c.wait()
    z_done(1, half_c, DEPTH - 1)
    side_c = cross(1, half_c, end_c)
    own_d.wait()
    z_done(2, half_d, DEPTH - 1)
    side_d = cross(2, half_d, end_d)

    def home(block):
        return block.astype(F32).reshape(BLOCK, BLOCK).T

    def finish_value(index, carry):
        cols = columns(index)
        dv_ref[:, cols] = (home(end_c[index]) * g_ref[:, cols].astype(F32)).astype(BF16)
        return carry

    xy_done(1, end_c, side_c)
    lax.fori_loop(0, COLS, finish_value, 0)
    away_v = pltpu.make_async_copy(dv_ref, dv_out, leave.at[0])
    away_v.start()

    def finish_gates(index, carry):
        cols = columns(index)
        back = home(end_d[index])
        dq_ref[:, cols] = (back * k_ref[:, cols].astype(F32)).astype(BF16)
        dk_ref[:, cols] = (back * q_ref[:, cols].astype(F32)).astype(BF16)
        return carry

    xy_done(2, end_d, side_d)
    lax.fori_loop(0, COLS, finish_gates, 0)
    away_q = pltpu.make_async_copy(dq_ref, dq_out, leave.at[1])
    away_q.start()
    away_k = pltpu.make_async_copy(dk_ref, dk_out, leave.at[2])
    away_k.start()

    def finish_filter(index, carry):
        block = end_l[pl.ds(index * DEPTH, DEPTH)]
        df_ref[:, columns(index)] = home(block).astype(BF16)
        return carry

    far_done(2, end_l, own_l)
    lax.fori_loop(0, COLS, finish_filter, 0)
    away_f = pltpu.make_async_copy(df_ref, df_out, leave.at[3])
    away_f.start()

    for kind in range(3):
        part = mid_f.at[pl.ds(0, 7)] if kind == 0 else half_c.at[pl.ds(0, DEPTH - 1)]
        z_copy(kind, part, part, depths[1]).wait_send()
        part = (got_f if kind == 0 else end_c).at[pl.ds(0, COLS - 1)]
        xy_copy(kind, part, part, beside(1)).wait_send()
        part = got_p.at[pl.ds(0, COLS * DEPTH - 1)]
        far_copy(kind, part, part, col, depths[1]).wait_send()
    for copy in (away_v, away_q, away_k, away_f):
        copy.wait()


def settle(*refs):
    sources, targets, stops, (into, onward) = refs[:4], refs[4:8], refs[8:12], refs[12:]
    arrivals = [pltpu.make_async_copy(sources[n], stops[n], into.at[n]) for n in range(4)]
    for copy in arrivals:
        copy.start()
    leaving = [pltpu.make_async_copy(stops[n], targets[n], onward.at[n]) for n in range(4)]
    for first, second in zip(arrivals, leaving, strict=True):
        first.wait()
        second.start()
    for copy in leaving:
        copy.wait()


def per_device(query_proj, key_proj, value_proj, out_grad, raw_filter):
    shape = jax.ShapeDtypeStruct(query_proj.shape, BF16)
    full = pltpu.VMEM((COLS, DEPTH, OWN, BLOCK), BF16)
    half = pltpu.VMEM((COLS, DEPTH // 2, OWN, BLOCK), BF16)
    near = pltpu.VMEM((DEPTH // 2, COLS, OWN, BLOCK), BF16)
    flat = pltpu.VMEM((COLS * DEPTH, OWN, BLOCK), BF16)
    consts = tuple(jnp.asarray(table) for table in tables())
    whole = pltpu.VMEM(query_proj.shape, BF16)
    spectra = pltpu.VMEM((OWN // 2, 2 * LONG, 2 * BLOCK), F32)
    anywhere = pl.BlockSpec(memory_space=pl.ANY)
    outs = pl.pallas_call(
        kernel,
        out_shape=(shape,) * 4,
        in_specs=[anywhere] * (5 + len(consts)),
        out_specs=(anywhere,) * 4,
        scratch_shapes=[
            *([whole] * 5),
            *(pltpu.VMEM(table.shape, table.dtype) for table in consts),
            *([whole] * 4),
            full, near, half, flat, flat, flat, flat,
            full, full, full, full, full, full, half, flat,
            pltpu.VMEM((COLS * DEPTH * OWN, BLOCK), F32),
            spectra, spectra,
            *([pltpu.SemaphoreType.DMA((3,))] * 6),
            pltpu.SemaphoreType.DMA((9,)),
            pltpu.SemaphoreType.DMA((10,)),
            pltpu.SemaphoreType.DMA((4,)),
            pltpu.SemaphoreType.REGULAR,
        ],
        compiler_params=pltpu.CompilerParams(
            collective_id=0, has_side_effects=True, vmem_limit_bytes=60 * 1024 * 1024
        ),
    )(query_proj, key_proj, value_proj, out_grad, raw_filter, *consts)
    return pl.pallas_call(
        settle,
        out_shape=(shape,) * 4,
        in_specs=[anywhere] * 4,
        out_specs=(anywhere,) * 4,
        scratch_shapes=[*([whole] * 4), *([pltpu.SemaphoreType.DMA((4,))] * 2)],
        compiler_params=pltpu.CompilerParams(vmem_limit_bytes=60 * 1024 * 1024),
    )(*outs)


def solution(mesh):
    in_specs = (P("ctx", "tp"), P("ctx", "tp"), P("ctx", "tp"), P("ctx", "tp"), P("ctx", None))
    out_specs = (P("ctx", "tp"), P("ctx", "tp"), P("ctx", "tp"), P("ctx", None))
    return jax.shard_map(
        per_device, mesh=mesh, in_specs=in_specs, out_specs=out_specs, check_vma=False
    )
```

```python
import functools
import math

import jax
import jax.numpy as jnp
import ml_dtypes
import numpy as np
from jax import lax
from jax.experimental import pallas as pl
from jax.experimental.pallas import tpu as pltpu
from jax.sharding import PartitionSpec as P

MESH = pl.DeviceIdType.MESH
BF16 = jnp.bfloat16
F32 = jnp.float32

BLOCK = 128
LONG = 256
PERIOD = BLOCK * LONG
COLS = 16
DEPTH = 16
OWN = 8


def split_table(table):
    high = table.astype(ml_dtypes.bfloat16)
    low = (table - high.astype(np.float64)).astype(ml_dtypes.bfloat16)
    return np.stack([high, low])


def tables():
    freq = np.arange(LONG)[:, None]
    block = np.arange(BLOCK)[None, :]
    long_angle = 2.0 * math.pi * ((freq * block) % LONG) / LONG
    cos_long, sin_long = np.cos(long_angle), np.sin(long_angle)
    outer = np.block([[cos_long, sin_long], [-sin_long, cos_long]])
    small_angle = 2.0 * math.pi * ((block.T * block) % BLOCK) / BLOCK
    cos_small, sin_small = np.cos(small_angle), np.sin(small_angle)
    inner = np.block([[cos_small, -sin_small], [sin_small, cos_small]])
    twid_angle = 2.0 * math.pi * (freq * block) / PERIOD
    turn = np.stack([np.cos(twid_angle), np.sin(twid_angle)]).astype(np.float32)
    return (*(split_table(table) for table in (outer, inner, inner.T, outer.T)), turn)


def mul(left, right):
    return jnp.dot(left, right, preferred_element_type=F32)


def halves(value):
    high = value.astype(BF16)
    return high, (value - high.astype(F32)).astype(BF16)


def kernel(
    q_in, k_in, v_in, g_in, f_in, out_in, inn_in, back_in, last_in, turn_in,
    dq_ref, dk_ref, dv_ref, df_ref,
    q_ref, k_ref, v_ref, g_ref, f_ref, out_tab, inn_tab, back_tab, last_tab, turn_tab,
    cut_f, mid_f, got_f, cut_p, got_p, cut_g, got_g,
    send_c, half_c, end_c, send_d, end_d, send_l, end_l,
    wide, spec_h, spec_p,
    z_send, z_recv, xy_send, xy_recv, far_send, far_recv, loc, fetch, ready,
):
    ctx, tp = lax.axis_index("ctx"), lax.axis_index("tp")
    col = ctx // 8
    low = ctx % 8
    zc = tp * 8 + low
    z, core = zc // 2, zc % 2
    me = col * DEPTH + zc

    def device(there, depth):
        return (there * 8 + depth % 8, depth // 8)

    def around(step):
        return lax.rem(zc + step, DEPTH)

    def beside(step):
        across = lax.rem(col % 4 + step % 4, 4)
        along = lax.rem(col // 4 + step // 4, 4)
        return along * 4 + across

    depths = [around(step) for step in range(DEPTH)]
    barrier = pltpu.get_barrier_semaphore()

    def greet(step, carry):
        for target in (device(col, around(step)), device(beside(step), zc)):
            pl.semaphore_signal(barrier, inc=1, device_id=target, device_id_type=MESH)
        return carry

    lax.fori_loop(1, 16, greet, 0)

    arrivals = [
        pltpu.make_async_copy(src, dst, fetch.at[n])
        for n, (src, dst) in enumerate(
            (
                (f_in, f_ref), (q_in, q_ref), (k_in, k_ref), (g_in, g_ref), (v_in, v_ref),
                (out_in, out_tab), (inn_in, inn_tab), (back_in, back_tab),
                (last_in, last_tab), (turn_in, turn_tab),
            )
        )
    ]
    for copy in arrivals:
        copy.start()

    def z_copy(kind, src, dst, index):
        return pltpu.make_async_remote_copy(
            src_ref=src, dst_ref=dst, send_sem=z_send.at[kind], recv_sem=z_recv.at[kind],
            device_id=device(col, index), device_id_type=MESH,
        )

    def xy_copy(kind, src, dst, index):
        return pltpu.make_async_remote_copy(
            src_ref=src, dst_ref=dst, send_sem=xy_send.at[kind], recv_sem=xy_recv.at[kind],
            device_id=device(index, zc), device_id_type=MESH,
        )

    def far_copy(kind, src, dst, there, depth):
        return pltpu.make_async_remote_copy(
            src_ref=src, dst_ref=dst, send_sem=far_send.at[kind], recv_sem=far_recv.at[kind],
            device_id=device(there, depth), device_id_type=MESH,
        )

    def columns(index):
        return pl.ds(pl.multiple_of(index * BLOCK, BLOCK), BLOCK)

    def turned(block):
        return block.T.astype(BF16).reshape(DEPTH, OWN, BLOCK)

    arrivals[0].wait()

    def cut_filter(index, carry):
        cut_f[index] = turned(f_ref[:, columns(index)].astype(F32))
        return carry

    lax.fori_loop(0, COLS, cut_filter, 0)
    pl.semaphore_wait(barrier, 30)

    def announce(step, carry):
        target = device(beside(step), zc)
        pl.semaphore_signal(ready, inc=1, device_id=target, device_id_type=MESH)
        return carry

    lax.fori_loop(1, COLS, announce, 0)
    flip = lax.rem(col // 4 + col + core, 2)

    def send_filter(step, carry):
        turn = step // 2
        away = jnp.where(turn == 3, jnp.where(flip == 0, 2, 6), jnp.where(turn == 2, 7, turn))
        index = lax.rem(z + away, 8) * 2 + lax.rem(core + step, 2)
        z_copy(0, cut_f.at[:, index], mid_f.at[low], index).start()
        return carry

    lax.fori_loop(1, 8, send_filter, 0)
    own_f = pltpu.make_async_copy(cut_f.at[:, zc], mid_f.at[low], loc.at[0])
    own_f.start()

    def cut_block(kind, step, left, right, cut, got):
        there = beside(step)
        cols = columns(there)
        product = left[:, cols].astype(F32) * right[:, cols].astype(F32)
        cut[pl.ds(there * DEPTH, DEPTH)] = turned(product.astype(BF16).astype(F32))
        return there

    def send_block(kind, there, depths, cut, got):
        for depth in depths:
            far_copy(kind, cut.at[there * DEPTH + depth], got.at[me], there, depth).start()

    def cut_product(kind, left, right, cut, got, before):
        there = cut_block(kind, 0, left, right, cut, got)
        send_block(kind, there, depths[1:], cut, got)
        before()

        def one(step, carry):
            there = cut_block(kind, step, left, right, cut, got)
            send_block(kind, there, depths, cut, got)
            return carry

        lax.fori_loop(1, COLS, one, 0)
        own = pltpu.make_async_copy(cut.at[me], got.at[me], loc.at[kind + 1])
        own.start()
        return own

    def far_done(kind, got, own):
        own.wait()
        part = got.at[pl.ds(0, COLS * DEPTH - 1)]
        far_copy(kind, part, part, col, depths[1]).wait_recv()

    def z_done(kind, mid, count):
        part = mid.at[pl.ds(0, count)]
        z_copy(kind, part, part, depths[1]).wait_recv()

    def cross(kind, mid, got):
        def one(step, carry):
            index = beside(step)
            xy_copy(kind, mid.at[:, index], got.at[col], index).start()
            return carry

        lax.fori_loop(1, COLS, one, 0)
        own = pltpu.make_async_copy(mid.at[:, col], got.at[col], loc.at[kind + 3])
        own.start()
        return own

    def xy_done(kind, got, own):
        own.wait()
        part = got.at[pl.ds(0, COLS - 1)]
        xy_copy(kind, part, part, beside(1)).wait_recv()

    arrivals[1].wait()
    arrivals[2].wait()
    own_p = cut_product(0, q_ref, k_ref, cut_p, got_p, lambda: pl.semaphore_wait(ready, COLS - 1))
    own_f.wait()
    z_done(0, mid_f, 7)
    side_f = cross(0, mid_f, got_f)
    arrivals[3].wait()
    arrivals[4].wait()
    own_g = cut_product(1, g_ref, v_ref, cut_g, got_g, lambda: None)
    for copy in arrivals[5:]:
        copy.wait()

    cos, sin = turn_tab[0], turn_tab[1]
    cos2 = jnp.concatenate([cos, cos], axis=1)
    sin2 = jnp.concatenate([sin, sin], axis=1)

    def forward(sig, depth):
        first = mul(out_tab[0, :, :depth], sig) + mul(out_tab[1, :, :depth], sig)
        real, imag = first[:LONG], first[LONG:]
        tr = real * cos2 + imag * sin2
        ti = imag * cos2 - real * sin2
        rows = jnp.concatenate(
            [
                jnp.concatenate([tr[:, :BLOCK], ti[:, :BLOCK]], axis=1),
                jnp.concatenate([tr[:, BLOCK:], ti[:, BLOCK:]], axis=1),
            ],
            axis=0,
        )
        hi, lo = halves(rows)
        return mul(hi, inn_tab[0]) + mul(hi, inn_tab[1]) + mul(lo, inn_tab[0])

    def inverse(spec, rows):
        hi, lo = halves(spec)
        mixed = mul(hi, back_tab[0]) + mul(hi, back_tab[1]) + mul(lo, back_tab[0])
        real = jnp.concatenate([mixed[:LONG, :BLOCK], mixed[LONG:, :BLOCK]], axis=1)
        imag = jnp.concatenate([mixed[:LONG, BLOCK:], mixed[LONG:, BLOCK:]], axis=1)
        both = jnp.concatenate([real * cos2 - imag * sin2, real * sin2 + imag * cos2], axis=0)
        hi, lo = halves(both)
        total = (
            mul(last_tab[0, :rows], hi) + mul(last_tab[1, :rows], hi) + mul(last_tab[0, :rows], lo)
        )
        return total * (1.0 / PERIOD / BLOCK)

    def times(left, right, conjugate):
        lr, li = left[:, :BLOCK], left[:, BLOCK:]
        rr, ri = right[:, :BLOCK], right[:, BLOCK:]
        if conjugate:
            return jnp.concatenate([lr * rr + li * ri, lr * ri - li * rr], axis=1)
        return jnp.concatenate([lr * rr - li * ri, lr * ri + li * rr], axis=1)

    def load(base, jump):
        parts = [wide[pl.ds(base + n * jump, 8, stride=OWN), :] for n in range(COLS)]
        return jnp.concatenate(parts, axis=0).astype(BF16)

    def store(base, jump, value):
        for n in range(COLS):
            wide[pl.ds(base + n * jump, 8, stride=OWN), :] = value[n * 8 : n * 8 + 8]

    def load_pair(one):
        top = [load(one, BLOCK), load(one + 1, BLOCK)]
        bottom = [load(one + 64, BLOCK), load(one + 65, BLOCK)]
        return jnp.concatenate(
            [jnp.concatenate(top, axis=1), jnp.concatenate(bottom, axis=1)], axis=0
        )

    def store_pair(one, value):
        store(one, BLOCK, value[:BLOCK, :BLOCK])
        store(one + 1, BLOCK, value[:BLOCK, BLOCK:])
        store(one + 64, BLOCK, value[BLOCK:, :BLOCK])
        store(one + 65, BLOCK, value[BLOCK:, BLOCK:])

    def spread(got):
        value = got[...].astype(F32)
        rows = value.size // BLOCK
        wide[pl.ds(0, rows), :] = value.reshape(rows, BLOCK)

    def gather(out):
        rows = out.shape[0] * out.shape[1] * OWN
        out[...] = wide[pl.ds(0, rows), :].astype(BF16).reshape(out.shape)

    xy_done(0, got_f, side_f)
    spread(got_f)

    def filter_spectrum(pair, carry):
        one = 2 * pair
        sig = jnp.concatenate([load(one, 64), load(one + 1, 64)], axis=1)
        spec_h[pair] = forward(sig, BLOCK)
        return carry

    lax.fori_loop(0, OWN // 2, filter_spectrum, 0, unroll=2)

    far_done(0, got_p, own_p)
    spread(got_p)

    def convolve(pair, carry):
        spec = forward(load_pair(2 * pair), 2 * BLOCK)
        spec_p[pair] = spec
        store_pair(2 * pair, inverse(times(spec_h[pair], spec, False), 2 * BLOCK))
        return carry

    lax.fori_loop(0, OWN // 2, convolve, 0, unroll=2)
    gather(send_c)

    def deliver(kind, out, mid):
        def one(step, carry):
            index = around(step)
            z_copy(kind, out.at[:, index], mid.at[zc], index).start()
            return carry

        lax.fori_loop(1, DEPTH, one, 0)
        own = pltpu.make_async_copy(out.at[:, zc], mid.at[zc], loc.at[kind + 5])
        own.start()
        return own

    own_c = deliver(1, send_c, half_c)

    far_done(1, got_g, own_g)
    spread(got_g)

    def correlate(pair, carry):
        spec = forward(load_pair(2 * pair), 2 * BLOCK)
        store_pair(2 * pair, inverse(times(spec_h[pair], spec, True), 2 * BLOCK))
        spec_p[pair] = times(spec_p[pair], spec, True)
        return carry

    lax.fori_loop(0, OWN // 2, correlate, 0, unroll=2)
    gather(send_d)

    def deliver_far(kind, out, end):
        def send(there, depths):
            for depth in depths:
                src = out.at[there, depth % out.shape[1]]
                far_copy(kind, src, end.at[me], there, depth).start()

        def one(step, carry):
            send(beside(step), depths)
            return carry

        send(col, depths[1:])
        lax.fori_loop(1, COLS, one, 0)
        own = pltpu.make_async_copy(out.at[col, lax.rem(zc, out.shape[1])], end.at[me], loc.at[kind + 5])
        own.start()
        return own

    own_d = deliver_far(2, send_d, end_d)

    def lag(pair, carry):
        value = inverse(spec_p[pair], BLOCK)
        store(2 * pair, 64, value[:, :BLOCK])
        store(2 * pair + 1, 64, value[:, BLOCK:])
        return carry

    lax.fori_loop(0, OWN // 2, lag, 0, unroll=2)
    gather(send_l)

    own_l = deliver_far(3, send_l, end_l)

    own_c.wait()
    z_done(1, half_c, DEPTH - 1)
    side_c = cross(1, half_c, end_c)

    def home(block):
        return block.astype(F32).reshape(BLOCK, BLOCK).T

    def finish_value(index, carry):
        cols = columns(index)
        dv_ref[:, cols] = (home(end_c[index]) * g_ref[:, cols].astype(F32)).astype(BF16)
        return carry

    def finish_gates(index, carry):
        cols = columns(index)
        back = home(end_d[pl.ds(index * DEPTH, DEPTH)])
        dq_ref[:, cols] = (back * k_ref[:, cols].astype(F32)).astype(BF16)
        dk_ref[:, cols] = (back * q_ref[:, cols].astype(F32)).astype(BF16)
        return carry

    xy_done(1, end_c, side_c)
    lax.fori_loop(0, COLS, finish_value, 0)
    far_done(2, end_d, own_d)
    lax.fori_loop(0, COLS, finish_gates, 0)

    def finish_filter(index, carry):
        block = end_l[pl.ds(index * DEPTH, DEPTH)]
        df_ref[:, columns(index)] = home(block).astype(BF16)
        return carry

    far_done(3, end_l, own_l)
    lax.fori_loop(0, COLS, finish_filter, 0)

    for kind in range(2):
        part = mid_f.at[pl.ds(0, 7)] if kind == 0 else half_c.at[pl.ds(0, DEPTH - 1)]
        z_copy(kind, part, part, depths[1]).wait_send()
        part = (got_f if kind == 0 else end_c).at[pl.ds(0, COLS - 1)]
        xy_copy(kind, part, part, beside(1)).wait_send()
    for kind in range(4):
        part = got_p.at[pl.ds(0, COLS * DEPTH - 1)]
        far_copy(kind, part, part, col, depths[1]).wait_send()


def settle(*refs):
    copies = [pltpu.make_async_copy(refs[n], refs[n + 4], refs[8].at[n]) for n in range(4)]
    for copy in copies:
        copy.start()
    for copy in copies:
        copy.wait()


def per_device(query_proj, key_proj, value_proj, out_grad, raw_filter):
    shape = jax.ShapeDtypeStruct(query_proj.shape, BF16)
    full = pltpu.VMEM((COLS, DEPTH, OWN, BLOCK), BF16)
    half = pltpu.VMEM((COLS, DEPTH // 2, OWN, BLOCK), BF16)
    near = pltpu.VMEM((DEPTH // 2, COLS, OWN, BLOCK), BF16)
    flat = pltpu.VMEM((COLS * DEPTH, OWN, BLOCK), BF16)
    consts = tuple(jnp.asarray(table) for table in tables())
    whole = pltpu.VMEM(query_proj.shape, BF16)
    spectra = pltpu.VMEM((OWN // 2, 2 * LONG, 2 * BLOCK), F32)
    anywhere = pl.BlockSpec(memory_space=pl.ANY)
    outs = pl.pallas_call(
        kernel,
        out_shape=(pltpu.VMEM(query_proj.shape, BF16),) * 4,
        in_specs=[anywhere] * (5 + len(consts)),
        out_specs=(pl.BlockSpec(memory_space=pltpu.VMEM),) * 4,
        scratch_shapes=[
            *([whole] * 5),
            *(pltpu.VMEM(table.shape, table.dtype) for table in consts),
            full, near, half, flat, flat, flat, flat,
            full, full, full, full, flat, half, flat,
            pltpu.VMEM((COLS * DEPTH * OWN, BLOCK), F32),
            spectra, spectra,
            *([pltpu.SemaphoreType.DMA((2,))] * 4),
            *([pltpu.SemaphoreType.DMA((4,))] * 2),
            pltpu.SemaphoreType.DMA((9,)),
            pltpu.SemaphoreType.DMA((10,)),
            pltpu.SemaphoreType.REGULAR,
        ],
        compiler_params=pltpu.CompilerParams(
            collective_id=0, has_side_effects=True, vmem_limit_bytes=58 * 1024 * 1024
        ),
    )(query_proj, key_proj, value_proj, out_grad, raw_filter, *consts)
    return pl.pallas_call(
        settle,
        out_shape=(shape,) * 4,
        in_specs=[anywhere] * 4,
        out_specs=(anywhere,) * 4,
        scratch_shapes=[pltpu.SemaphoreType.DMA((4,))],
        compiler_params=pltpu.CompilerParams(vmem_limit_bytes=1024 * 1024),
    )(*outs)


def solution(mesh):
    in_specs = (P("ctx", "tp"), P("ctx", "tp"), P("ctx", "tp"), P("ctx", "tp"), P("ctx", None))
    out_specs = (P("ctx", "tp"), P("ctx", "tp"), P("ctx", "tp"), P("ctx", None))
    return jax.shard_map(
        per_device, mesh=mesh, in_specs=in_specs, out_specs=out_specs, check_vma=False
    )
```

```python
import functools
import math

import jax
import jax.numpy as jnp
import ml_dtypes
import numpy as np
from jax import lax
from jax.experimental import pallas as pl
from jax.experimental.pallas import tpu as pltpu
from jax.sharding import PartitionSpec as P

MESH = pl.DeviceIdType.MESH
BF16 = jnp.bfloat16
F32 = jnp.float32

BLOCK = 128
LONG = 256
PERIOD = BLOCK * LONG
COLS = 16
DEPTH = 16
OWN = 8


def split_table(table):
    high = table.astype(ml_dtypes.bfloat16)
    low = (table - high.astype(np.float64)).astype(ml_dtypes.bfloat16)
    return np.stack([high, low])


def tables():
    freq = np.arange(LONG)[:, None]
    block = np.arange(BLOCK)[None, :]
    long_angle = 2.0 * math.pi * ((freq * block) % LONG) / LONG
    cos_long, sin_long = np.cos(long_angle), np.sin(long_angle)
    outer = np.block([[cos_long, sin_long], [-sin_long, cos_long]])
    small_angle = 2.0 * math.pi * ((block.T * block) % BLOCK) / BLOCK
    cos_small, sin_small = np.cos(small_angle), np.sin(small_angle)
    inner = np.block([[cos_small, -sin_small], [sin_small, cos_small]])
    twid_angle = 2.0 * math.pi * (freq * block) / PERIOD
    turn = np.stack([np.cos(twid_angle), np.sin(twid_angle)]).astype(np.float32)
    return (*(split_table(table) for table in (outer, inner, inner.T, outer.T)), turn)


def mul(left, right):
    return jnp.dot(left, right, preferred_element_type=F32)


def halves(value):
    high = value.astype(BF16)
    return high, (value - high.astype(F32)).astype(BF16)


def kernel(
    q_in, k_in, v_in, g_in, f_in, out_in, inn_in, back_in, last_in, turn_in,
    dq_ref, dk_ref, dv_ref, df_ref,
    q_ref, k_ref, v_ref, g_ref, f_ref, out_tab, inn_tab, back_tab, last_tab, turn_tab,
    cut_f, mid_f, got_f, cut_p, got_p, cut_g, got_g,
    send_c, end_c, send_d, end_d, send_l, end_l,
    wide, spec_h, spec_p,
    z_send, z_recv, xy_send, xy_recv, far_send, far_recv, loc, fetch, ready,
):
    ctx, tp = lax.axis_index("ctx"), lax.axis_index("tp")
    col = ctx // 8
    low = ctx % 8
    zc = tp * 8 + low
    z, core = zc // 2, zc % 2
    me = col * DEPTH + zc

    def device(there, depth):
        return (there * 8 + depth % 8, depth // 8)

    def around(step):
        return lax.rem(zc + step, DEPTH)

    def beside(step):
        across = lax.rem(col % 4 + step % 4, 4)
        along = lax.rem(col // 4 + step // 4, 4)
        return along * 4 + across

    def distant(step):
        along, across = 3 - step // 4, 3 - step % 4
        turns = [jnp.where(n == 2, 3, jnp.where(n == 3, 2, n)) for n in (along, across)]
        return turns[0] * 4 + turns[1]

    hops = (8, 9, 6, 11, 7, 10, 4, 13, 5, 12, 2, 15, 3, 14, 1)
    depths = [around(step) for step in hops]
    everyone = [*depths, zc]
    barrier = pltpu.get_barrier_semaphore()

    def greet(target):
        pl.semaphore_signal(barrier, inc=1, device_id=target, device_id_type=MESH)

    for step, depth in enumerate(depths):
        greet(device(col, depth))
        greet(device(beside(distant(step)), zc))

    arrivals = [
        pltpu.make_async_copy(src, dst, fetch.at[n])
        for n, (src, dst) in enumerate(
            (
                (f_in, f_ref), (q_in, q_ref), (k_in, k_ref), (g_in, g_ref), (v_in, v_ref),
                (out_in, out_tab), (inn_in, inn_tab), (back_in, back_tab),
                (last_in, last_tab), (turn_in, turn_tab),
            )
        )
    ]
    for copy in arrivals:
        copy.start()

    def z_copy(kind, src, dst, index):
        return pltpu.make_async_remote_copy(
            src_ref=src, dst_ref=dst, send_sem=z_send.at[kind], recv_sem=z_recv.at[kind],
            device_id=device(col, index), device_id_type=MESH,
        )

    def xy_copy(kind, src, dst, index):
        return pltpu.make_async_remote_copy(
            src_ref=src, dst_ref=dst, send_sem=xy_send.at[kind], recv_sem=xy_recv.at[kind],
            device_id=device(index, zc), device_id_type=MESH,
        )

    def far_copy(kind, src, dst, there, depth, part=0):
        return pltpu.make_async_remote_copy(
            src_ref=src, dst_ref=dst, send_sem=far_send.at[kind], recv_sem=far_recv.at[kind + part],
            device_id=device(there, depth), device_id_type=MESH,
        )

    def columns(index):
        return pl.ds(pl.multiple_of(index * BLOCK, BLOCK), BLOCK)

    def turned(block):
        return block.T.astype(BF16).reshape(DEPTH, OWN, BLOCK)

    arrivals[0].wait()

    def cut_filter(index, carry):
        cut_f[index] = turned(f_ref[:, columns(index)].astype(F32))
        return carry

    lax.fori_loop(0, COLS, cut_filter, 0)
    pl.semaphore_wait(barrier, 30)

    for step in range(COLS - 1):
        target = device(beside(distant(step)), zc)
        pl.semaphore_signal(ready, inc=1, device_id=target, device_id_type=MESH)
    flip = lax.rem(col // 4 + col + core, 2)

    def send_filter(step, carry):
        turn = step // 2
        away = jnp.where(turn == 3, jnp.where(flip == 0, 2, 6), jnp.where(turn == 2, 7, turn))
        index = lax.rem(z + away, 8) * 2 + lax.rem(core + step, 2)
        z_copy(0, cut_f.at[:, index], mid_f.at[low], index).start()
        return carry

    lax.fori_loop(0, 7, lambda n, carry: send_filter(7 - n, carry), 0)
    own_f = pltpu.make_async_copy(cut_f.at[:, zc], mid_f.at[low], loc.at[0])
    own_f.start()

    def cut_product(left, right, cut):
        def one(there, carry):
            cols = columns(there)
            product = left[:, cols].astype(F32) * right[:, cols].astype(F32)
            cut[pl.ds(there * DEPTH, DEPTH)] = turned(product.astype(BF16).astype(F32))
            return carry

        lax.fori_loop(0, COLS, one, 0)

    def send_block(kind, there, depths, cut, got):
        for depth in depths:
            far_copy(kind, cut.at[there * DEPTH + depth], got.at[me], there, depth).start()

    def send_product(kind, cut, got):
        def one(step, carry):
            send_block(kind, beside(distant(step)), everyone, cut, got)
            return carry

        lax.fori_loop(0, COLS - 1, one, 0)
        own = pltpu.make_async_copy(cut.at[me], got.at[me], loc.at[kind + 1])
        own.start()
        return own

    def far_done(kind, got, own):
        own.wait()
        part = got.at[pl.ds(0, COLS * DEPTH - 1)]
        far_copy(kind, part, part, col, depths[0]).wait_recv()

    def z_done(kind, mid, count):
        part = mid.at[pl.ds(0, count)]
        z_copy(kind, part, part, depths[0]).wait_recv()

    def cross(kind, mid, got):
        def one(step, carry):
            index = beside(distant(step))
            xy_copy(kind, mid.at[:, index], got.at[col], index).start()
            return carry

        lax.fori_loop(0, COLS - 1, one, 0)
        own = pltpu.make_async_copy(mid.at[:, col], got.at[col], loc.at[7])
        own.start()
        return own

    def xy_done(kind, got, own):
        own.wait()
        part = got.at[pl.ds(0, COLS - 1)]
        xy_copy(kind, part, part, beside(distant(0))).wait_recv()

    arrivals[1].wait()
    arrivals[2].wait()
    cut_product(q_ref, k_ref, cut_p)
    send_block(0, col, depths, cut_p, got_p)
    arrivals[3].wait()
    arrivals[4].wait()
    cut_product(g_ref, v_ref, cut_g)
    pl.semaphore_wait(ready, COLS - 1)
    own_p = send_product(0, cut_p, got_p)
    own_f.wait()
    z_done(0, mid_f, 7)
    side_f = cross(0, mid_f, got_f)
    own_g = send_product(1, cut_g, got_g)
    send_block(1, col, depths, cut_g, got_g)
    for copy in arrivals[5:]:
        copy.wait()

    cos, sin = turn_tab[0], turn_tab[1]
    cos2 = jnp.concatenate([cos, cos], axis=1)
    sin2 = jnp.concatenate([sin, sin], axis=1)

    def forward(sig, depth):
        first = mul(out_tab[0, :, :depth], sig) + mul(out_tab[1, :, :depth], sig)
        real, imag = first[:LONG], first[LONG:]
        tr = real * cos2 + imag * sin2
        ti = imag * cos2 - real * sin2
        rows = jnp.concatenate(
            [
                jnp.concatenate([tr[:, :BLOCK], ti[:, :BLOCK]], axis=1),
                jnp.concatenate([tr[:, BLOCK:], ti[:, BLOCK:]], axis=1),
            ],
            axis=0,
        )
        hi, lo = halves(rows)
        return mul(hi, inn_tab[0]) + mul(hi, inn_tab[1]) + mul(lo, inn_tab[0])

    def inverse(spec, rows):
        hi, lo = halves(spec)
        mixed = mul(hi, back_tab[0]) + mul(hi, back_tab[1]) + mul(lo, back_tab[0])
        real = jnp.concatenate([mixed[:LONG, :BLOCK], mixed[LONG:, :BLOCK]], axis=1)
        imag = jnp.concatenate([mixed[:LONG, BLOCK:], mixed[LONG:, BLOCK:]], axis=1)
        both = jnp.concatenate([real * cos2 - imag * sin2, real * sin2 + imag * cos2], axis=0)
        hi, lo = halves(both)
        total = (
            mul(last_tab[0, :rows], hi) + mul(last_tab[1, :rows], hi) + mul(last_tab[0, :rows], lo)
        )
        return total * (1.0 / PERIOD / BLOCK)

    def times(left, right, conjugate):
        lr, li = left[:, :BLOCK], left[:, BLOCK:]
        rr, ri = right[:, :BLOCK], right[:, BLOCK:]
        if conjugate:
            return jnp.concatenate([lr * rr + li * ri, lr * ri - li * rr], axis=1)
        return jnp.concatenate([lr * rr - li * ri, lr * ri + li * rr], axis=1)

    def load(base, jump):
        parts = [wide[pl.ds(base + n * jump, 8, stride=OWN), :] for n in range(COLS)]
        return jnp.concatenate(parts, axis=0).astype(BF16)

    def store(base, jump, value):
        for n in range(COLS):
            wide[pl.ds(base + n * jump, 8, stride=OWN), :] = value[n * 8 : n * 8 + 8]

    def load_pair(one):
        top = [load(one, BLOCK), load(one + 1, BLOCK)]
        bottom = [load(one + 64, BLOCK), load(one + 65, BLOCK)]
        return jnp.concatenate(
            [jnp.concatenate(top, axis=1), jnp.concatenate(bottom, axis=1)], axis=0
        )

    def store_pair(one, value):
        store(one, BLOCK, value[:BLOCK, :BLOCK])
        store(one + 1, BLOCK, value[:BLOCK, BLOCK:])
        store(one + 64, BLOCK, value[BLOCK:, :BLOCK])
        store(one + 65, BLOCK, value[BLOCK:, BLOCK:])

    def spread(got):
        value = got[...].astype(F32)
        rows = value.size // BLOCK
        wide[pl.ds(0, rows), :] = value.reshape(rows, BLOCK)

    def gather(out):
        rows = out.shape[0] * out.shape[1] * OWN
        out[...] = wide[pl.ds(0, rows), :].astype(BF16).reshape(out.shape)

    xy_done(0, got_f, side_f)
    spread(got_f)

    def filter_spectrum(pair, carry):
        one = 2 * pair
        sig = jnp.concatenate([load(one, 64), load(one + 1, 64)], axis=1)
        spec_h[pair] = forward(sig, BLOCK)
        return carry

    lax.fori_loop(0, OWN // 2, filter_spectrum, 0, unroll=4)

    far_done(0, got_p, own_p)
    spread(got_p)

    def convolve(pair, carry):
        spec = forward(load_pair(2 * pair), 2 * BLOCK)
        spec_p[pair] = spec
        store_pair(2 * pair, inverse(times(spec_h[pair], spec, False), 2 * BLOCK))
        return carry

    lax.fori_loop(0, OWN // 2, convolve, 0, unroll=4)
    gather(send_c)

    def deliver_far(kind, out, end):
        def send(there, depths, part):
            for depth in depths:
                src = out.at[there, depth % out.shape[1]]
                far_copy(kind, src, end.at[me], there, depth, part).start()

        def one(step, carry):
            send(beside(distant(step)), everyone, step // 4 if kind == 4 else 0)
            return carry

        lax.fori_loop(0, COLS - 1, one, 0)
        send(col, depths, 3 if kind == 4 else 0)
        own = pltpu.make_async_copy(out.at[col, lax.rem(zc, out.shape[1])], end.at[me], loc.at[kind + 2])
        own.start()
        return own

    own_c = deliver_far(2, send_c, end_c)

    far_done(1, got_g, own_g)
    spread(got_g)

    def correlate(pair, carry):
        spec = forward(load_pair(2 * pair), 2 * BLOCK)
        store_pair(2 * pair, inverse(times(spec_h[pair], spec, True), 2 * BLOCK))
        spec_p[pair] = times(spec_p[pair], spec, True)
        return carry

    lax.fori_loop(0, OWN // 2, correlate, 0, unroll=4)
    gather(send_d)

    own_d = deliver_far(3, send_d, end_d)

    def lag(pair, carry):
        value = inverse(spec_p[pair], BLOCK)
        store(2 * pair, 64, value[:, :BLOCK])
        store(2 * pair + 1, 64, value[:, BLOCK:])
        return carry

    lax.fori_loop(0, OWN // 2, lag, 0, unroll=4)
    gather(send_l)

    own_l = deliver_far(4, send_l, end_l)

    def home(block):
        return block.astype(F32).reshape(BLOCK, BLOCK).T

    def finish_value(index, carry):
        cols = columns(index)
        dv_ref[:, cols] = (home(end_c[pl.ds(index * DEPTH, DEPTH)]) * g_ref[:, cols].astype(F32)).astype(BF16)
        return carry

    def finish_gates(index, carry):
        cols = columns(index)
        back = home(end_d[pl.ds(index * DEPTH, DEPTH)])
        dq_ref[:, cols] = (back * k_ref[:, cols].astype(F32)).astype(BF16)
        dk_ref[:, cols] = (back * q_ref[:, cols].astype(F32)).astype(BF16)
        return carry

    far_done(2, end_c, own_c)
    lax.fori_loop(0, COLS, finish_value, 0)
    far_done(3, end_d, own_d)
    lax.fori_loop(0, COLS, finish_gates, 0)

    def finish_filter(index, carry):
        block = end_l[pl.ds(index * DEPTH, DEPTH)]
        df_ref[:, columns(index)] = home(block).astype(BF16)
        return carry

    own_l.wait()
    for part in range(4):
        some = end_l.at[pl.ds(0, 4 * DEPTH - (part == 3))]
        far_copy(4, some, some, col, depths[0], part).wait_recv()
        row = lax.rem(col // 4 + 4 - distant(4 * part) // 4, 4)
        for n in range(4):
            finish_filter(row * 4 + n, 0)

    part = mid_f.at[pl.ds(0, 7)]
    z_copy(0, part, part, depths[0]).wait_send()
    part = got_f.at[pl.ds(0, COLS - 1)]
    xy_copy(0, part, part, beside(distant(0))).wait_send()
    for kind in range(5):
        part = got_p.at[pl.ds(0, COLS * DEPTH - 1)]
        far_copy(kind, part, part, col, depths[0]).wait_send()


def settle(*refs):
    copies = [pltpu.make_async_copy(refs[n], refs[n + 4], refs[8].at[n]) for n in range(4)]
    for copy in copies:
        copy.start()
    for copy in copies:
        copy.wait()


def per_device(query_proj, key_proj, value_proj, out_grad, raw_filter):
    shape = jax.ShapeDtypeStruct(query_proj.shape, BF16)
    full = pltpu.VMEM((COLS, DEPTH, OWN, BLOCK), BF16)
    half = pltpu.VMEM((COLS, DEPTH // 2, OWN, BLOCK), BF16)
    near = pltpu.VMEM((DEPTH // 2, COLS, OWN, BLOCK), BF16)
    flat = pltpu.VMEM((COLS * DEPTH, OWN, BLOCK), BF16)
    consts = tuple(jnp.asarray(table) for table in tables())
    whole = pltpu.VMEM(query_proj.shape, BF16)
    spectra = pltpu.VMEM((OWN // 2, 2 * LONG, 2 * BLOCK), F32)
    anywhere = pl.BlockSpec(memory_space=pl.ANY)
    outs = pl.pallas_call(
        kernel,
        out_shape=(pltpu.VMEM(query_proj.shape, BF16),) * 4,
        in_specs=[anywhere] * (5 + len(consts)),
        out_specs=(pl.BlockSpec(memory_space=pltpu.VMEM),) * 4,
        scratch_shapes=[
            *([whole] * 5),
            *(pltpu.VMEM(table.shape, table.dtype) for table in consts),
            full, near, half, flat, flat, flat, flat,
            full, flat, full, flat, half, flat,
            pltpu.VMEM((COLS * DEPTH * OWN, BLOCK), F32),
            spectra, spectra,
            *([pltpu.SemaphoreType.DMA((1,))] * 4),
            pltpu.SemaphoreType.DMA((5,)),
            pltpu.SemaphoreType.DMA((8,)),
            pltpu.SemaphoreType.DMA((8,)),
            pltpu.SemaphoreType.DMA((10,)),
            pltpu.SemaphoreType.REGULAR,
        ],
        compiler_params=pltpu.CompilerParams(
            collective_id=0, has_side_effects=True, vmem_limit_bytes=58 * 1024 * 1024
        ),
    )(query_proj, key_proj, value_proj, out_grad, raw_filter, *consts)
    return pl.pallas_call(
        settle,
        out_shape=(shape,) * 4,
        in_specs=[anywhere] * 4,
        out_specs=(anywhere,) * 4,
        scratch_shapes=[pltpu.SemaphoreType.DMA((4,))],
        compiler_params=pltpu.CompilerParams(vmem_limit_bytes=1024 * 1024),
    )(*outs)


def solution(mesh):
    in_specs = (P("ctx", "tp"), P("ctx", "tp"), P("ctx", "tp"), P("ctx", "tp"), P("ctx", None))
    out_specs = (P("ctx", "tp"), P("ctx", "tp"), P("ctx", "tp"), P("ctx", None))
    return jax.shard_map(
        per_device, mesh=mesh, in_specs=in_specs, out_specs=out_specs, check_vma=False
    )
```

```python
import functools
import math

import jax
import jax.numpy as jnp
import ml_dtypes
import numpy as np
from jax import lax
from jax.experimental import pallas as pl
from jax.experimental.pallas import tpu as pltpu
from jax.sharding import PartitionSpec as P

MESH = pl.DeviceIdType.MESH
BF16 = jnp.bfloat16
F32 = jnp.float32

BLOCK = 128
LONG = 256
PERIOD = BLOCK * LONG
COLS = 16
DEPTH = 16
OWN = 8


def split_table(table):
    high = table.astype(ml_dtypes.bfloat16)
    low = (table - high.astype(np.float64)).astype(ml_dtypes.bfloat16)
    return np.stack([high, low])


def tables():
    freq = np.arange(LONG)[:, None]
    block = np.arange(BLOCK)[None, :]
    long_angle = 2.0 * math.pi * ((freq * block) % LONG) / LONG
    cos_long, sin_long = np.cos(long_angle), np.sin(long_angle)
    outer = np.block([[cos_long, sin_long], [-sin_long, cos_long]])
    small_angle = 2.0 * math.pi * ((block.T * block) % BLOCK) / BLOCK
    cos_small, sin_small = np.cos(small_angle), np.sin(small_angle)
    inner = np.block([[cos_small, -sin_small], [sin_small, cos_small]])
    twid_angle = 2.0 * math.pi * (freq * block) / PERIOD
    turn = np.stack([np.cos(twid_angle), np.sin(twid_angle)]).astype(np.float32)
    return (*(split_table(table) for table in (outer, inner, inner.T, outer.T)), turn)


def mul(left, right):
    return jnp.dot(left, right, preferred_element_type=F32)


def halves(value):
    high = value.astype(BF16)
    return high, (value - high.astype(F32)).astype(BF16)


def kernel(
    q_in, k_in, v_in, g_in, f_in, out_in, inn_in, back_in, last_in, turn_in,
    dq_ref, dk_ref, dv_ref, df_ref,
    q_ref, k_ref, v_ref, g_ref, f_ref, out_tab, inn_tab, back_tab, last_tab, turn_tab,
    cut_f, mid_f, got_f, cut_p, got_p, cut_g, got_g,
    send_c, end_c, send_d, end_d, send_l, end_l,
    wide, spec_h, spec_p,
    z_send, z_recv, xy_send, xy_recv, far_send, far_recv, loc, fetch, ready,
):
    ctx, tp = lax.axis_index("ctx"), lax.axis_index("tp")
    col = ctx // 8
    low = ctx % 8
    zc = tp * 8 + low
    z, core = zc // 2, zc % 2
    me = col * DEPTH + zc

    def device(there, depth):
        return (there * 8 + depth % 8, depth // 8)

    def around(step):
        return lax.rem(zc + step, DEPTH)

    def beside(step):
        across = lax.rem(col % 4 + step % 4, 4)
        along = lax.rem(col // 4 + step // 4, 4)
        return along * 4 + across

    def distant(step):
        along, across = 3 - step // 4, 3 - step % 4
        turns = [jnp.where(n == 2, 3, jnp.where(n == 3, 2, n)) for n in (along, across)]
        return turns[0] * 4 + turns[1]

    hops = (8, 2, 14, 6, 10, 4, 12, 9, 3, 15, 7, 11, 5, 13, 1)
    depths = [around(step) for step in hops]
    everyone = [*depths, zc]
    barrier = pltpu.get_barrier_semaphore()

    def greet(target):
        pl.semaphore_signal(barrier, inc=1, device_id=target, device_id_type=MESH)

    for step, depth in enumerate(depths):
        greet(device(col, depth))
        greet(device(beside(distant(step)), zc))

    arrivals = [
        pltpu.make_async_copy(src, dst, fetch.at[n])
        for n, (src, dst) in enumerate(
            (
                (f_in, f_ref), (q_in, q_ref), (k_in, k_ref), (g_in, g_ref), (v_in, v_ref),
                (out_in, out_tab), (inn_in, inn_tab), (back_in, back_tab),
                (last_in, last_tab), (turn_in, turn_tab),
            )
        )
    ]
    for copy in arrivals:
        copy.start()

    def z_copy(kind, src, dst, index):
        return pltpu.make_async_remote_copy(
            src_ref=src, dst_ref=dst, send_sem=z_send.at[kind], recv_sem=z_recv.at[kind],
            device_id=device(col, index), device_id_type=MESH,
        )

    def xy_copy(kind, src, dst, index):
        return pltpu.make_async_remote_copy(
            src_ref=src, dst_ref=dst, send_sem=xy_send.at[kind], recv_sem=xy_recv.at[kind],
            device_id=device(index, zc), device_id_type=MESH,
        )

    def far_copy(kind, src, dst, there, depth, part=0):
        return pltpu.make_async_remote_copy(
            src_ref=src, dst_ref=dst, send_sem=far_send.at[kind], recv_sem=far_recv.at[kind + part],
            device_id=device(there, depth), device_id_type=MESH,
        )

    def columns(index):
        return pl.ds(pl.multiple_of(index * BLOCK, BLOCK), BLOCK)

    def turned(block):
        return block.T.astype(BF16).reshape(DEPTH, OWN, BLOCK)

    arrivals[0].wait()

    def cut_filter(index, carry):
        cut_f[index] = turned(f_ref[:, columns(index)].astype(F32))
        return carry

    lax.fori_loop(0, COLS, cut_filter, 0)
    pl.semaphore_wait(barrier, 30)

    for step in range(COLS - 1):
        target = device(beside(distant(step)), zc)
        pl.semaphore_signal(ready, inc=1, device_id=target, device_id_type=MESH)
    flip = lax.rem(col // 4 + col + core, 2)

    def send_filter(step, carry):
        turn = step // 2
        away = jnp.where(turn == 3, jnp.where(flip == 0, 2, 6), jnp.where(turn == 2, 7, turn))
        index = lax.rem(z + away, 8) * 2 + lax.rem(core + step, 2)
        z_copy(0, cut_f.at[:, index], mid_f.at[low], index).start()
        return carry

    lax.fori_loop(0, 7, lambda n, carry: send_filter(7 - n, carry), 0)
    own_f = pltpu.make_async_copy(cut_f.at[:, zc], mid_f.at[low], loc.at[0])
    own_f.start()

    def cut_product(left, right, cut):
        def one(there, carry):
            cols = columns(there)
            product = left[:, cols].astype(F32) * right[:, cols].astype(F32)
            cut[pl.ds(there * DEPTH, DEPTH)] = turned(product.astype(BF16).astype(F32))
            return carry

        lax.fori_loop(0, COLS, one, 0)

    def send_block(kind, there, depths, cut, got):
        for depth in depths:
            far_copy(kind, cut.at[there * DEPTH + depth], got.at[me], there, depth).start()

    def send_product(kind, cut, got):
        def one(step, carry):
            send_block(kind, beside(distant(step)), everyone, cut, got)
            return carry

        lax.fori_loop(0, COLS - 1, one, 0)
        own = pltpu.make_async_copy(cut.at[me], got.at[me], loc.at[kind + 1])
        own.start()
        return own

    def far_done(kind, got, own):
        own.wait()
        part = got.at[pl.ds(0, COLS * DEPTH - 1)]
        far_copy(kind, part, part, col, depths[0]).wait_recv()

    def z_done(kind, mid, count):
        part = mid.at[pl.ds(0, count)]
        z_copy(kind, part, part, depths[0]).wait_recv()

    def cross(kind, mid, got):
        def one(step, carry):
            index = beside(distant(step))
            xy_copy(kind, mid.at[:, index], got.at[col], index).start()
            return carry

        lax.fori_loop(0, COLS - 1, one, 0)
        own = pltpu.make_async_copy(mid.at[:, col], got.at[col], loc.at[7])
        own.start()
        return own

    def xy_done(kind, got, own):
        own.wait()
        part = got.at[pl.ds(0, COLS - 1)]
        xy_copy(kind, part, part, beside(distant(0))).wait_recv()

    arrivals[1].wait()
    arrivals[2].wait()
    cut_product(q_ref, k_ref, cut_p)
    send_block(0, col, depths, cut_p, got_p)
    pl.semaphore_wait(ready, COLS - 1)
    own_p = send_product(0, cut_p, got_p)
    arrivals[3].wait()
    arrivals[4].wait()
    cut_product(g_ref, v_ref, cut_g)
    own_f.wait()
    z_done(0, mid_f, 7)
    side_f = cross(0, mid_f, got_f)
    own_g = send_product(1, cut_g, got_g)
    send_block(1, col, depths, cut_g, got_g)
    for copy in arrivals[5:]:
        copy.wait()

    cos, sin = turn_tab[0], turn_tab[1]
    cos2 = jnp.concatenate([cos, cos], axis=1)
    sin2 = jnp.concatenate([sin, sin], axis=1)

    def forward(sig, depth):
        first = mul(out_tab[0, :, :depth], sig) + mul(out_tab[1, :, :depth], sig)
        real, imag = first[:LONG], first[LONG:]
        tr = real * cos2 + imag * sin2
        ti = imag * cos2 - real * sin2
        rows = jnp.concatenate(
            [
                jnp.concatenate([tr[:, :BLOCK], ti[:, :BLOCK]], axis=1),
                jnp.concatenate([tr[:, BLOCK:], ti[:, BLOCK:]], axis=1),
            ],
            axis=0,
        )
        hi, lo = halves(rows)
        return mul(hi, inn_tab[0]) + mul(hi, inn_tab[1]) + mul(lo, inn_tab[0])

    def inverse(spec, rows):
        hi, lo = halves(spec)
        mixed = mul(hi, back_tab[0]) + mul(hi, back_tab[1]) + mul(lo, back_tab[0])
        real = jnp.concatenate([mixed[:LONG, :BLOCK], mixed[LONG:, :BLOCK]], axis=1)
        imag = jnp.concatenate([mixed[:LONG, BLOCK:], mixed[LONG:, BLOCK:]], axis=1)
        both = jnp.concatenate([real * cos2 - imag * sin2, real * sin2 + imag * cos2], axis=0)
        hi, lo = halves(both)
        total = (
            mul(last_tab[0, :rows], hi) + mul(last_tab[1, :rows], hi) + mul(last_tab[0, :rows], lo)
        )
        return total * (1.0 / PERIOD / BLOCK)

    def times(left, right, conjugate):
        lr, li = left[:, :BLOCK], left[:, BLOCK:]
        rr, ri = right[:, :BLOCK], right[:, BLOCK:]
        if conjugate:
            return jnp.concatenate([lr * rr + li * ri, lr * ri - li * rr], axis=1)
        return jnp.concatenate([lr * rr - li * ri, lr * ri + li * rr], axis=1)

    def load(base, jump):
        parts = [wide[pl.ds(base + n * jump, 8, stride=OWN), :] for n in range(COLS)]
        return jnp.concatenate(parts, axis=0).astype(BF16)

    def store(base, jump, value):
        for n in range(COLS):
            wide[pl.ds(base + n * jump, 8, stride=OWN), :] = value[n * 8 : n * 8 + 8]

    def load_pair(one):
        top = [load(one, BLOCK), load(one + 1, BLOCK)]
        bottom = [load(one + 64, BLOCK), load(one + 65, BLOCK)]
        return jnp.concatenate(
            [jnp.concatenate(top, axis=1), jnp.concatenate(bottom, axis=1)], axis=0
        )

    def store_pair(one, value):
        store(one, BLOCK, value[:BLOCK, :BLOCK])
        store(one + 1, BLOCK, value[:BLOCK, BLOCK:])
        store(one + 64, BLOCK, value[BLOCK:, :BLOCK])
        store(one + 65, BLOCK, value[BLOCK:, BLOCK:])

    def spread(got):
        value = got[...].astype(F32)
        rows = value.size // BLOCK
        wide[pl.ds(0, rows), :] = value.reshape(rows, BLOCK)

    def gather(out):
        rows = out.shape[0] * out.shape[1] * OWN
        out[...] = wide[pl.ds(0, rows), :].astype(BF16).reshape(out.shape)

    xy_done(0, got_f, side_f)
    spread(got_f)

    def filter_spectrum(pair, carry):
        one = 2 * pair
        sig = jnp.concatenate([load(one, 64), load(one + 1, 64)], axis=1)
        spec_h[pair] = forward(sig, BLOCK)
        return carry

    lax.fori_loop(0, OWN // 2, filter_spectrum, 0, unroll=4)

    far_done(0, got_p, own_p)
    spread(got_p)

    def convolve(pair, carry):
        spec = forward(load_pair(2 * pair), 2 * BLOCK)
        spec_p[pair] = spec
        store_pair(2 * pair, inverse(times(spec_h[pair], spec, False), 2 * BLOCK))
        return carry

    lax.fori_loop(0, OWN // 2, convolve, 0, unroll=4)
    gather(send_c)

    def deliver_far(kind, out, end):
        def send(there, depths, part):
            for depth in depths:
                src = out.at[there, depth % out.shape[1]]
                far_copy(kind, src, end.at[me], there, depth, part).start()

        def one(step, carry):
            send(beside(distant(step)), everyone, step // 4 if kind == 4 else 0)
            return carry

        lax.fori_loop(0, COLS - 1, one, 0)
        send(col, depths, 3 if kind == 4 else 0)
        own = pltpu.make_async_copy(out.at[col, lax.rem(zc, out.shape[1])], end.at[me], loc.at[kind + 2])
        own.start()
        return own

    own_c = deliver_far(2, send_c, end_c)

    far_done(1, got_g, own_g)
    spread(got_g)

    def correlate(pair, carry):
        spec = forward(load_pair(2 * pair), 2 * BLOCK)
        store_pair(2 * pair, inverse(times(spec_h[pair], spec, True), 2 * BLOCK))
        spec_p[pair] = times(spec_p[pair], spec, True)
        return carry

    lax.fori_loop(0, OWN // 2, correlate, 0, unroll=4)
    gather(send_d)

    own_d = deliver_far(3, send_d, end_d)

    def lag(pair, carry):
        value = inverse(spec_p[pair], BLOCK)
        store(2 * pair, 64, value[:, :BLOCK])
        store(2 * pair + 1, 64, value[:, BLOCK:])
        return carry

    lax.fori_loop(0, OWN // 2, lag, 0, unroll=4)
    gather(send_l)

    own_l = deliver_far(4, send_l, end_l)

    def home(block):
        return block.astype(F32).reshape(BLOCK, BLOCK).T

    def finish_value(index, carry):
        cols = columns(index)
        dv_ref[:, cols] = (home(end_c[pl.ds(index * DEPTH, DEPTH)]) * g_ref[:, cols].astype(F32)).astype(BF16)
        return carry

    def finish_gates(index, carry):
        cols = columns(index)
        back = home(end_d[pl.ds(index * DEPTH, DEPTH)])
        dq_ref[:, cols] = (back * k_ref[:, cols].astype(F32)).astype(BF16)
        dk_ref[:, cols] = (back * q_ref[:, cols].astype(F32)).astype(BF16)
        return carry

    far_done(2, end_c, own_c)
    lax.fori_loop(0, COLS, finish_value, 0)
    far_done(3, end_d, own_d)
    lax.fori_loop(0, COLS, finish_gates, 0)

    def finish_filter(index, carry):
        block = end_l[pl.ds(index * DEPTH, DEPTH)]
        df_ref[:, columns(index)] = home(block).astype(BF16)
        return carry

    own_l.wait()
    for part in range(4):
        some = end_l.at[pl.ds(0, 4 * DEPTH - (part == 3))]
        far_copy(4, some, some, col, depths[0], part).wait_recv()
        row = lax.rem(col // 4 + 4 - distant(4 * part) // 4, 4)
        for n in range(4):
            finish_filter(row * 4 + n, 0)

    part = mid_f.at[pl.ds(0, 7)]
    z_copy(0, part, part, depths[0]).wait_send()
    part = got_f.at[pl.ds(0, COLS - 1)]
    xy_copy(0, part, part, beside(distant(0))).wait_send()
    for kind in range(5):
        part = got_p.at[pl.ds(0, COLS * DEPTH - 1)]
        far_copy(kind, part, part, col, depths[0]).wait_send()


def settle(*refs):
    copies = [pltpu.make_async_copy(refs[n], refs[n + 4], refs[8].at[n]) for n in range(4)]
    for copy in copies:
        copy.start()
    for copy in copies:
        copy.wait()


def per_device(query_proj, key_proj, value_proj, out_grad, raw_filter):
    shape = jax.ShapeDtypeStruct(query_proj.shape, BF16)
    full = pltpu.VMEM((COLS, DEPTH, OWN, BLOCK), BF16)
    half = pltpu.VMEM((COLS, DEPTH // 2, OWN, BLOCK), BF16)
    near = pltpu.VMEM((DEPTH // 2, COLS, OWN, BLOCK), BF16)
    flat = pltpu.VMEM((COLS * DEPTH, OWN, BLOCK), BF16)
    consts = tuple(jnp.asarray(table) for table in tables())
    whole = pltpu.VMEM(query_proj.shape, BF16)
    spectra = pltpu.VMEM((OWN // 2, 2 * LONG, 2 * BLOCK), F32)
    anywhere = pl.BlockSpec(memory_space=pl.ANY)
    outs = pl.pallas_call(
        kernel,
        out_shape=(pltpu.VMEM(query_proj.shape, BF16),) * 4,
        in_specs=[anywhere] * (5 + len(consts)),
        out_specs=(pl.BlockSpec(memory_space=pltpu.VMEM),) * 4,
        scratch_shapes=[
            *([whole] * 5),
            *(pltpu.VMEM(table.shape, table.dtype) for table in consts),
            full, near, half, flat, flat, flat, flat,
            full, flat, full, flat, half, flat,
            pltpu.VMEM((COLS * DEPTH * OWN + 8 * OWN, BLOCK), F32),
            spectra, spectra,
            *([pltpu.SemaphoreType.DMA((1,))] * 4),
            pltpu.SemaphoreType.DMA((5,)),
            pltpu.SemaphoreType.DMA((8,)),
            pltpu.SemaphoreType.DMA((8,)),
            pltpu.SemaphoreType.DMA((10,)),
            pltpu.SemaphoreType.REGULAR,
        ],
        compiler_params=pltpu.CompilerParams(
            collective_id=0, has_side_effects=True, vmem_limit_bytes=58 * 1024 * 1024
        ),
    )(query_proj, key_proj, value_proj, out_grad, raw_filter, *consts)
    return pl.pallas_call(
        settle,
        out_shape=(shape,) * 4,
        in_specs=[anywhere] * 4,
        out_specs=(anywhere,) * 4,
        scratch_shapes=[pltpu.SemaphoreType.DMA((4,))],
        compiler_params=pltpu.CompilerParams(vmem_limit_bytes=1024 * 1024),
    )(*outs)


def solution(mesh):
    in_specs = (P("ctx", "tp"), P("ctx", "tp"), P("ctx", "tp"), P("ctx", "tp"), P("ctx", None))
    out_specs = (P("ctx", "tp"), P("ctx", "tp"), P("ctx", "tp"), P("ctx", None))
    return jax.shard_map(
        per_device, mesh=mesh, in_specs=in_specs, out_specs=out_specs, check_vma=False
    )
```
